256 devices in a mesh: pair: 64 (over x, z, core), red: 4 (over y).
Axes of the slice: x: 4, y: 4, z: 8, core: 2. Of those that a mesh axis runs over, the one named last changes fastest.
Arguments:
- integrals: bfloat16 [2048, 64, 1536], P(('pair', 'red')), may hold values from -6 to 6
- coeffs: bfloat16 [6016, 512], replicated, may hold values from -0.078125 to 0.078125
- shell_pairs: int32 [2048, 2], replicated, may hold values from 0 to 93, as said below
- block_count: int32 [64, 4], P('pair', 'red'), may hold values from 1 to 8, as said below
Outputs:
- mo_ints: float32 [512, 24, 512], P('pair', None, 'red')
The draws below stay inside these ranges and needn't reach their ends.
Inputs may be any that keep to these rules, and one draw needn't show every extreme that they name: `shell_pairs`: the 2048 rows are distinct shell pairs (row shell, column shell). `block_count`: some device has all 8 slots live.
All inputs are finite; a program needn't handle non-finite values.
Results may differ from the reference program's by a relative error of at most 0.0029.
Values may be sent and summed in bfloat16 or wider, within the bound.
No kernel may reach another device: no remote copies, remote signals or barrier semaphores. Data moves between devices by JAX's collectives and lax.ppermute only.
A program may use at most 128 MiB of HBM per device.

```python
import jax
import jax.numpy as jnp
from jax import lax

SHELL_WIDTH = 64
SHELL_BLOCKS = 94
NAO = 6016
OCCUPIED_COUNT = 512
KET_PAIRS = 24
BLK_CAP = 8
TOTAL_SLOTS = 2048
N_PAIR = 64
N_RED = 4


def draw_shell_pairs(key, part):
    key = jax.random.fold_in(key, 11)
    selected_blocks = jax.random.permutation(key, SHELL_BLOCKS * SHELL_BLOCKS)[:TOTAL_SLOTS]
    return jnp.stack([selected_blocks // SHELL_BLOCKS, selected_blocks % SHELL_BLOCKS], axis=1).astype(jnp.int32)


def draw_block_count(key, part):
    key = jax.random.fold_in(key, 23)
    first_key, second_key = jax.random.split(key)
    counts = jax.random.randint(first_key, (N_PAIR * N_RED,), 1, BLK_CAP + 1)
    fullest = jax.random.randint(second_key, (), 0, N_PAIR * N_RED)
    counts = jnp.where(jnp.arange(N_PAIR * N_RED) == fullest, BLK_CAP, counts)
    return counts.reshape(N_PAIR, N_RED).astype(jnp.int32)


def shard_levels(stream_key, dims, cuts, least, top_value):
    factor_of, own = 1.0, jax.random.fold_in(stream_key, 6)
    for axis_at, shards_of in cuts:
        steps = jnp.exp(jax.random.uniform(jax.random.fold_in(own, axis_at), (shards_of,), jnp.float32, least / len(cuts), top_value / len(cuts)))
        factor_of = factor_of * jnp.repeat(steps, dims[axis_at] // shards_of).reshape([-1 if axis == axis_at else 1 for axis in range(len(dims))])
    return factor_of


def bell_draw(key, extent, spread, most, shards=(), held_as=jnp.bfloat16):
    level = shard_levels(key, extent, shards, -0.22, 0.18) if shards else 1.0
    result = jax.random.normal(key, extent, jnp.float32) * spread * level
    return jnp.minimum(jnp.maximum(result, -most), most).astype(held_as)


def setup_inputs(seed: int = 0) -> dict:
    keys = jax.random.split(jax.random.key(seed), 5)
    return {
        "integrals": bell_draw(keys[0], (TOTAL_SLOTS, SHELL_WIDTH, KET_PAIRS * SHELL_WIDTH), 1.0, 6.0, ((0, 256),)),
        "coeffs": bell_draw(keys[1], (NAO, OCCUPIED_COUNT), NAO ** -0.5, 0.078125),
        "shell_pairs": draw_shell_pairs(jax.random.fold_in(keys[4], 71), 0),
        "block_count": draw_block_count(jax.random.fold_in(keys[4], 71), 0),
    }


def reference(integrals, coeffs, shell_pairs, block_count):
    live_counts = block_count.reshape(-1)
    coef_table = coeffs.reshape(SHELL_BLOCKS, SHELL_WIDTH, OCCUPIED_COUNT).astype(jnp.float32)

    def block_adder(collected_blocks, slot_index):
        row_shell = shell_pairs[slot_index, 0]
        col_shell = shell_pairs[slot_index, 1]
        live_mask = ((slot_index % BLK_CAP) < live_counts[slot_index // BLK_CAP]).astype(jnp.float32)
        left_panel = lax.dynamic_index_in_dim(coef_table, row_shell, 0, keepdims=False)
        tile_block = lax.dynamic_index_in_dim(integrals, slot_index, 0, keepdims=False).astype(jnp.float32)
        half_done = jnp.dot(left_panel.T, tile_block, precision=lax.Precision.HIGHEST) * live_mask
        half_done = lax.optimization_barrier(half_done.astype(jnp.bfloat16))
        half_done = half_done.astype(jnp.float32).reshape(OCCUPIED_COUNT * KET_PAIRS, SHELL_WIDTH)
        current = lax.dynamic_index_in_dim(collected_blocks, col_shell, 0, keepdims=False)
        collected_blocks = lax.dynamic_update_index_in_dim(collected_blocks, current + half_done, col_shell, 0)
        return collected_blocks, None

    collected_blocks, unused_value = lax.scan(block_adder, jnp.zeros((SHELL_BLOCKS, OCCUPIED_COUNT * KET_PAIRS, SHELL_WIDTH), jnp.float32), jnp.arange(TOTAL_SLOTS, dtype=jnp.int32))
    mo_flat = jnp.einsum("tan,tnj->aj", collected_blocks, coef_table, precision=lax.Precision.HIGHEST)
    return mo_flat.reshape(OCCUPIED_COUNT, KET_PAIRS, OCCUPIED_COUNT)
```

```python
import functools

import jax
import jax.numpy as jnp
from jax import lax
from jax.experimental import pallas as pl
from jax.experimental.pallas import tpu as pltpu
from jax.sharding import PartitionSpec as P

NX, NZ, NC, NY = 4, 8, 2, 4
SLOTS = 16
SH = 64
BF, F32 = jnp.bfloat16, jnp.float32


def pair_of(x, z, c):
    return (x * NZ + z) * NC + c


COORDS = [(x, z, c) for x in range(NX) for z in range(NZ) for c in range(NC)]


def move_x(a, d):
    return lax.ppermute(a, "pair", [(pair_of(x, z, c), pair_of((x + d) % NX, z, c)) for x, z, c in COORDS])


def move_z(a, d):
    return lax.ppermute(a, "pair", [(pair_of(x, z, c), pair_of(x, (z + d) % NZ, c)) for x, z, c in COORDS])


def move_y(a, d):
    return lax.ppermute(a, "red", [(y, (y + d) % NY) for y in range(NY)])


def swap_core(a):
    return lax.ppermute(a, "pair", [(pair_of(x, z, c), pair_of(x, z, 1 - c)) for x, z, c in COORDS])


def panel_kernel(idx, pos, coeffs, lt, r, lraw, lsem, rsem):
    x, z, c, y = pos[0], pos[1], pos[2], pos[3]
    copies_l, copies_r = [], []
    for k in range(SLOTS):
        row = pl.multiple_of(idx[0, k] * SH, SH)
        cp = pltpu.make_async_copy(coeffs.at[pl.ds(row, SH), :], lraw.at[pl.ds(k * SH, SH), :], lsem.at[k])
        cp.start()
        copies_l.append(cp)
    for k in range(SLOTS):
        row = pl.multiple_of(idx[1, k] * SH, SH)
        for yr in range(NY):
            col = pl.multiple_of(((y + yr) & (NY - 1)) * 128, 128)
            cp = pltpu.make_async_copy(
                coeffs.at[pl.ds(row, SH), pl.ds(col, 128)],
                r.at[pl.ds(k * SH, SH), pl.ds(yr * 128, 128)],
                rsem.at[k * NY + yr],
            )
            cp.start()
            copies_r.append(cp)
    ip = lax.broadcasted_iota(jnp.int32, (256, 512), 0)
    col = lax.broadcasted_iota(jnp.int32, (256, 512), 1)
    want = (((ip >> 6) + x) & 3) * 128 + ((((ip >> 3) & 7) + z) & 7) * 16 + c * 8 + (ip & 7)
    sel = jnp.where(col == want, 1.0, 0.0).astype(BF)
    for cp in copies_l:
        cp.wait()
    for g in range(4):
        lt[g] = lax.dot_general(
            sel, lraw[pl.ds(g * 256, 256), :], (((1,), (1,)), ((), ())), preferred_element_type=F32
        ).astype(BF)
    for cp in copies_r:
        cp.wait()


def panels(idx, pos, coeffs):
    return pl.pallas_call(
        panel_kernel,
        out_shape=(jax.ShapeDtypeStruct((4, 256, 256), BF), jax.ShapeDtypeStruct((1024, 512), BF)),
        in_specs=[
            pl.BlockSpec(memory_space=pltpu.SMEM),
            pl.BlockSpec(memory_space=pltpu.SMEM),
            pl.BlockSpec(memory_space=pl.ANY),
        ],
        out_specs=(pl.BlockSpec(memory_space=pltpu.VMEM), pl.BlockSpec(memory_space=pltpu.VMEM)),
        scratch_shapes=[
            pltpu.VMEM((1024, 512), BF),
            pltpu.SemaphoreType.DMA((SLOTS,)),
            pltpu.SemaphoreType.DMA((SLOTS * NY,)),
        ],
        cost_estimate=pl.CostEstimate(flops=300_000_000, bytes_accessed=4_000_000, transcendentals=0),
        name="panels",
    )(idx, pos, coeffs)


def block_kernel(by_x, acc_at, plain_at, cnt, lt_ref, r_ref, own_i, mate_i, far, plain, acc, own, lt, bd, half):
    step = pl.program_id(0)

    @pl.when(step == 0)
    def _():
        slot = lax.broadcasted_iota(jnp.int32, (256, 256), 1) >> 6
        for g in range(4):
            local = slot + 4 * (g % 2)
            keep = local < cnt[g // 2]
            lt[g] = jnp.where(keep, lt_ref[g].astype(F32), 0.0).astype(BF)
        bd[...] = jnp.zeros_like(bd)

    low = lax.broadcasted_iota(jnp.int32, (SH, 128), 1) < 64
    zero = jnp.zeros((SH, 128), F32)
    for k in range(SLOTS):
        src = (own_i if k < 8 else mate_i)[k % 8].astype(F32)
        swapped = pltpu.roll(src, 64, 1)
        g, kk = k // 4, k % 4
        for odd in range(2):
            piece = src if (kk % 2) == odd else swapped
            piece = jnp.where(low, zero, piece) if kk % 2 else jnp.where(low, piece, zero)
            bd[odd, g, pl.ds(kk * SH, SH), pl.ds((kk // 2) * 128, 128)] = piece.astype(BF)
    for odd in range(2):
        for g in range(4):
            half[pl.ds(odd * 256, 256), pl.ds(g * 256, 256)] = jnp.dot(
                lt[g], bd[odd, g], preferred_element_type=F32
            ).astype(BF)
    for odd in range(2):
        res = jnp.dot(half[pl.ds(odd * 256, 256), :], r_ref[...], preferred_element_type=F32)
        for at, ref in ((0, own), (2, far), (plain_at, plain), (acc_at, acc)):
            part = res[at * 64 : at * 64 + 64, :] if by_x else res[:, at * 128 : at * 128 + 128]
            ref[odd] = part.astype(ref.dtype)


def block(by_x, acc_at, plain_at, first_q, nq, cnt, lt, r, own_i, mate_i):
    rows, cols = (64, 512) if by_x else (256, 128)
    first = first_q // 2
    out = lambda dt: jax.ShapeDtypeStruct((nq, rows, cols), dt)
    spec = pl.BlockSpec((2, rows, cols), lambda s: (s, 0, 0))
    ints = pl.BlockSpec((8, SH, 128), lambda s: (0, 0, first + s))
    return pl.pallas_call(
        functools.partial(block_kernel, by_x, acc_at, plain_at),
        grid=(nq // 2,),
        out_shape=(out(BF), out(BF), out(F32), out(F32)),
        in_specs=[
            pl.BlockSpec(memory_space=pltpu.SMEM),
            pl.BlockSpec((4, 256, 256), lambda s: (0, 0, 0)),
            pl.BlockSpec((1024, 512), lambda s: (0, 0)),
            ints,
            ints,
        ],
        out_specs=(spec, spec, spec, spec),
        scratch_shapes=[
            pltpu.VMEM((4, 256, 256), BF),
            pltpu.VMEM((2, 4, 256, 256), BF),
            pltpu.VMEM((512, 1024), BF),
        ],
        compiler_params=pltpu.CompilerParams(vmem_limit_bytes=24 * 1024 * 1024),
        cost_estimate=pl.CostEstimate(flops=400_000_000 * nq, bytes_accessed=6_000_000, transcendentals=0),
        name="block_x" if by_x else "block_y",
    )(cnt, lt, r, own_i, mate_i)


def on_device(integrals, coeffs, shell_pairs, block_count):
    p = lax.axis_index("pair")
    y = lax.axis_index("red")
    x, z, c = p // (NZ * NC), (p // NC) % NZ, p % NC
    mate = p + 1 - 2 * c
    mate_i = swap_core(integrals)
    count = block_count[0, 0]
    mate_count = swap_core(block_count)[0, 0]
    own_sp = lax.dynamic_slice_in_dim(shell_pairs, (p * NY + y) * 8, 8, 0)
    mate_sp = lax.dynamic_slice_in_dim(shell_pairs, (mate * NY + y) * 8, 8, 0)
    idx = jnp.concatenate([own_sp, mate_sp], axis=0).T
    pos = jnp.stack([x, z, c, y]).astype(jnp.int32)
    cnt = jnp.stack([count, mate_count])
    lt, r = panels(idx, pos, coeffs)

    def parts(by_x, up, first_q):
        acc_at, plain_at = (1, 3) if up else (3, 1)
        return block(by_x, acc_at, plain_at, first_q, 6, cnt, lt, r, integrals, mate_i)

    def ring(by_x, up, made):
        far, plain, acc, own = made
        move = move_x if by_x else move_y
        d = 1 if up else -1
        got_far = move(far, d)
        got_plain = move(plain, -d)
        got_acc = move((acc + got_far.astype(F32)).astype(BF), d)
        return own + got_plain.astype(F32) + got_acc.astype(F32)

    made_xa = parts(True, True, 0)
    made_ya = parts(False, True, 12)
    made_xb = parts(True, False, 6)
    made_yb = parts(False, False, 18)
    sum_x = jnp.concatenate([ring(True, True, made_xa), ring(True, False, made_xb)], axis=0)
    sum_y = jnp.concatenate([ring(False, True, made_ya), ring(False, False, made_yb)], axis=0)

    tot_x, tot_y = sum_x[:, :, :128], sum_y[:, :64, :]
    for d in (1, 3, 2):
        tot_x = tot_x + move_y(sum_x[:, :, d * 128 : d * 128 + 128].astype(BF), d).astype(F32)
        tot_y = tot_y + move_x(sum_y[:, d * 64 : d * 64 + 64, :].astype(BF), d).astype(F32)
    tot = jnp.concatenate([tot_x, tot_y], axis=0).reshape(24, NZ, 8, 128)

    chunk = lambda d: tot[:, d % NZ]
    up, down = chunk(4), chunk(-3)
    for d in (3, 2, 1, 0):
        up = move_z(up, 1)
        if d:
            up = up + chunk(d)
            down = move_z(down, -1)
            if d > 1:
                down = down + chunk(1 - d)
    res = up + down + chunk(0)
    return jnp.transpose(res, (1, 0, 2))


def solution(mesh):
    return jax.shard_map(
        on_device,
        mesh=mesh,
        in_specs=(P(("pair", "red"), None, None), P(), P(), P("pair", "red")),
        out_specs=P("pair", None, "red"),
        check_vma=False,
    )
```

```python
import functools

import jax
import jax.numpy as jnp
from jax import lax
from jax.experimental import pallas as pl
from jax.experimental.pallas import tpu as pltpu
from jax.sharding import PartitionSpec as P

NX, NZ, NC, NY = 4, 8, 2, 4
SLOTS = 16
SH = 64
BF, F32 = jnp.bfloat16, jnp.float32
VMEM = 24 * 1024 * 1024
SIZES = (6, 6, 6, 6)


def pair_of(x, z, c):
    return (x * NZ + z) * NC + c


COORDS = [(x, z, c) for x in range(NX) for z in range(NZ) for c in range(NC)]


def move_x(a, d):
    return lax.ppermute(a, "pair", [(pair_of(x, z, c), pair_of((x + d) % NX, z, c)) for x, z, c in COORDS])


def trade_z(a):
    groups = [[pair_of(x, z, c) for z in range(NZ)] for x in range(NX) for c in range(NC)]
    return lax.all_to_all(a, "pair", 0, 0, tiled=True, axis_index_groups=groups)


def move_y(a, d):
    return lax.ppermute(a, "red", [(y, (y + d) % NY) for y in range(NY)])


def swap_core(a):
    return lax.ppermute(a, "pair", [(pair_of(x, z, c), pair_of(x, z, 1 - c)) for x, z, c in COORDS])


def panel_kernel(pairs, coeffs, lt, r, lraw, rraw, lsem, rsem):
    p, y = lax.axis_index("pair"), lax.axis_index("red")
    x, c = p >> 4, p & 1
    copies_l, copies_r = [], []
    for side, raw, sem, copies in ((0, lraw, lsem, copies_l), (1, rraw, rsem, copies_r)):
        for k in range(SLOTS):
            device = p if k < 8 else p + 1 - 2 * c
            row = pl.multiple_of(pairs[side, (device * NY + y) * 8 + k % 8] * SH, SH)
            cp = pltpu.make_async_copy(coeffs.at[pl.ds(row, SH), :], raw.at[pl.ds(k * SH, SH), :], sem.at[k])
            cp.start()
            copies.append(cp)
    ip = lax.broadcasted_iota(jnp.int32, (256, 512), 0)
    col = lax.broadcasted_iota(jnp.int32, (256, 512), 1)
    want = (((ip >> 6) + x) & 3) * 128 + ((ip >> 3) & 7) * 16 + c * 8 + (ip & 7)
    sel = jnp.where(col == want, 1.0, 0.0).astype(BF)
    for cp in copies_l:
        cp.wait()
    for g in range(4):
        lt[g] = lax.dot_general(
            sel, lraw[pl.ds(g * 256, 256), :], (((1,), (1,)), ((), ())), preferred_element_type=F32
        ).astype(BF)
    for cp in copies_r:
        cp.wait()
    for yr in range(NY):
        col = pl.multiple_of(((y + yr) & (NY - 1)) * 128, 128)
        r[:, pl.ds(yr * 128, 128)] = rraw[:, pl.ds(col, 128)]


def panels(pairs, coeffs):
    return pl.pallas_call(
        panel_kernel,
        out_shape=tuple(jax.ShapeDtypeStruct(dims, BF) for dims in ((4, 256, 256), (1024, 512))),
        in_specs=[pl.BlockSpec(memory_space=pltpu.SMEM), pl.BlockSpec(memory_space=pl.ANY)],
        out_specs=(pl.BlockSpec(memory_space=pltpu.VMEM),) * 2,
        scratch_shapes=[
            pltpu.VMEM((1024, 512), BF),
            pltpu.VMEM((1024, 512), BF),
            pltpu.SemaphoreType.DMA((SLOTS,)),
            pltpu.SemaphoreType.DMA((SLOTS,)),
        ],
        compiler_params=pltpu.CompilerParams(vmem_limit_bytes=2 * VMEM),
        cost_estimate=pl.CostEstimate(flops=300_000_000, bytes_accessed=4_000_000, transcendentals=0),
        name="panels",
    )(pairs, coeffs)


def block_kernel(by_x, acc_at, plain_at, own_n, mate_n, lt_ref, r_ref, own_i, mate_i, earlier, far, plain, acc, own, lt, bd, half):
    step = pl.program_id(0)

    @pl.when(step == 0)
    def _():
        slot = lax.broadcasted_iota(jnp.int32, (256, 256), 1) >> 6
        for g in range(4):
            local = slot + 4 * (g % 2)
            keep = local < (own_n if g < 2 else mate_n)[0, 0]
            lt[g] = jnp.where(keep, lt_ref[g].astype(F32), 0.0).astype(BF)
        bd[...] = jnp.zeros_like(bd)

    low = lax.broadcasted_iota(jnp.int32, (SH, 128), 1) < 64
    zero = jnp.zeros((SH, 128), F32)
    for k in range(SLOTS):
        src = (own_i if k < 8 else mate_i)[k % 8].astype(F32)
        swapped = pltpu.roll(src, 64, 1)
        g, kk = k // 4, k % 4
        for odd in range(2):
            piece = src if (kk % 2) == odd else swapped
            piece = jnp.where(low, zero, piece) if kk % 2 else jnp.where(low, piece, zero)
            bd[odd, g, pl.ds(kk * SH, SH), pl.ds((kk // 2) * 128, 128)] = piece.astype(BF)
    for odd in range(2):
        for g in range(4):
            half[pl.ds(odd * 256, 256), pl.ds(g * 256, 256)] = jnp.dot(
                lt[g], bd[odd, g], preferred_element_type=F32
            ).astype(BF)
    whole = jnp.dot(half[...], r_ref[...], preferred_element_type=F32)
    for odd in range(2):
        res = whole[odd * 256 : odd * 256 + 256]
        for at, ref in ((0, own), (2, far), (plain_at, plain), (acc_at, acc)):
            part = res[at * 64 : at * 64 + 64, :] if by_x else res[:, at * 128 : at * 128 + 128]
            ref[odd] = part.astype(ref.dtype)


def block(by_x, acc_at, plain_at, first_q, nq, earlier, own_n, mate_n, lt, r, own_i, mate_i):
    rows, cols = (64, 512) if by_x else (256, 128)
    first = first_q // 2
    out = lambda dt: jax.ShapeDtypeStruct((nq, rows, cols), dt)
    spec = pl.BlockSpec((2, rows, cols), lambda s: (s, 0, 0))
    ints = pl.BlockSpec((8, SH, 128), lambda s: (0, 0, first + s))
    return pl.pallas_call(
        functools.partial(block_kernel, by_x, acc_at, plain_at),
        grid=(nq // 2,),
        out_shape=(out(BF), out(BF), out(F32), out(F32)),
        in_specs=[
            pl.BlockSpec(memory_space=pltpu.SMEM),
            pl.BlockSpec(memory_space=pltpu.SMEM),
            pl.BlockSpec((4, 256, 256), lambda s: (0, 0, 0)),
            pl.BlockSpec((1024, 512), lambda s: (0, 0)),
            ints,
            ints,
            pl.BlockSpec(memory_space=pl.ANY),
        ],
        out_specs=(spec, spec, spec, spec),
        scratch_shapes=[
            pltpu.VMEM((4, 256, 256), BF),
            pltpu.VMEM((2, 4, 256, 256), BF),
            pltpu.VMEM((512, 1024), BF),
        ],
        compiler_params=pltpu.CompilerParams(vmem_limit_bytes=VMEM),
        cost_estimate=pl.CostEstimate(flops=1_000_000, bytes_accessed=10_000, transcendentals=0),
        name="block_x" if by_x else "block_y",
    )(own_n, mate_n, lt, r, own_i, mate_i, earlier)


def after(value, *earlier):
    return lax.optimization_barrier((value,) + earlier)[0]


def tie(*values):
    return lax.optimization_barrier(values)


def on_device(integrals, coeffs, shell_pairs, block_count):
    mate_i = swap_core(integrals)
    mate_n = swap_core(block_count)
    lt, r = panels(shell_pairs.T, coeffs)

    def parts(by_x, up, first_q, earlier, nq=6):
        acc_at, plain_at = (1, 3) if up else (3, 1)
        return block(by_x, acc_at, plain_at, first_q, nq, earlier, block_count, mate_n, lt, r, integrals, mate_i)

    def join(acc, far):
        return (acc + far.astype(F32)).astype(BF)

    def total(own, plain, acc):
        return own + plain.astype(F32) + acc.astype(F32)

    na, ma, nb, mb = SIZES
    far_xa, plain_xa, acc_xa, own_xa = parts(True, True, 0, lt, na)
    f_xa = move_x(far_xa, 1)
    p_xa = move_x(plain_xa, -1)
    far_ya, plain_ya, acc_ya, own_ya = parts(False, True, na + nb, own_xa, ma)
    f_ya = move_y(far_ya, 1)
    p_ya = move_y(plain_ya, -1)
    far_xb, plain_xb, acc_xb, own_xb = parts(True, False, na, own_ya, nb)
    far_xb, plain_xb, f_xa, p_xa, own_xb = tie(far_xb, plain_xb, f_xa, p_xa, own_xb)
    f_xb = move_x(far_xb, -1)
    p_xb = move_x(plain_xb, 1)
    far_yb, plain_yb, acc_yb, own_yb = parts(False, False, na + nb + ma, own_xb, mb)
    far_yb, plain_yb, f_ya, p_ya, own_yb = tie(far_yb, plain_yb, f_ya, p_ya, own_yb)
    f_yb = move_y(far_yb, -1)
    p_yb = move_y(plain_yb, 1)
    f_xa, f_xb, p_xb, own_yb = tie(f_xa, f_xb, p_xb, own_yb)
    a_xa = move_x(join(acc_xa, f_xa), 1)
    a_xb = move_x(join(acc_xb, f_xb), -1)
    f_ya, f_yb, p_yb = tie(f_ya, f_yb, p_yb)
    a_ya = move_y(join(acc_ya, f_ya), 1)
    a_yb = move_y(join(acc_yb, f_yb), -1)
    sum_x = jnp.concatenate([total(own_xa, p_xa, a_xa), total(own_xb, p_xb, a_xb)], axis=0)
    sum_y = jnp.concatenate([total(own_ya, p_ya, a_ya), total(own_yb, p_yb, a_yb)], axis=0)

    tot_x, tot_y = sum_x[:, :, :128], sum_y[:, :64, :]
    for d in (1, 3, 2):
        tot_x = tot_x + move_y(sum_x[:, :, d * 128 : d * 128 + 128].astype(BF), d).astype(F32)
        tot_y = tot_y + move_x(sum_y[:, d * 64 : d * 64 + 64, :].astype(BF), d).astype(F32)

    tot = jnp.concatenate([tot_x, tot_y], axis=0)
    send = jnp.transpose(tot.reshape(24, NZ, 8, 128), (1, 2, 0, 3))
    zi = (lax.axis_index("pair") // NC) % NZ
    own = lax.dynamic_index_in_dim(send, zi, 0, keepdims=False)
    got = trade_z(send.astype(BF))
    return jnp.where((jnp.arange(NZ) == zi)[:, None, None, None], own[None], got.astype(F32)).sum(0)


def solution(mesh):
    return jax.shard_map(
        on_device,
        mesh=mesh,
        in_specs=(P(("pair", "red"), None, None), P(), P(), P("pair", "red")),
        out_specs=P("pair", None, "red"),
        check_vma=False,
    )
```

```python
import functools

import jax
import jax.numpy as jnp
from jax import lax
from jax.experimental import pallas as pl
from jax.experimental.pallas import tpu as pltpu
from jax.sharding import PartitionSpec as P

NX, NZ, NC, NY = 4, 8, 2, 4
SLOTS = 16
SH = 64
BF, F32 = jnp.bfloat16, jnp.float32
VMEM = 24 * 1024 * 1024
SIZES = (6, 6, 6, 6)


def pair_of(x, z, c):
    return (x * NZ + z) * NC + c


COORDS = [(x, z, c) for x in range(NX) for z in range(NZ) for c in range(NC)]


def move_x(a, d):
    return lax.ppermute(a, "pair", [(pair_of(x, z, c), pair_of((x + d) % NX, z, c)) for x, z, c in COORDS])


def trade_z(a):
    groups = [[pair_of(x, z, c) for z in range(NZ)] for x in range(NX) for c in range(NC)]
    return lax.all_to_all(a, "pair", 0, 0, tiled=True, axis_index_groups=groups)


def move_y(a, d):
    return lax.ppermute(a, "red", [(y, (y + d) % NY) for y in range(NY)])


def swap_core(a):
    return lax.ppermute(a, "pair", [(pair_of(x, z, c), pair_of(x, z, 1 - c)) for x, z, c in COORDS])


def panel_kernel(pairs, coeffs, lt, r, lraw, rraw, lsem, rsem):
    p, y = lax.axis_index("pair"), lax.axis_index("red")
    x, c = p >> 4, p & 1
    copies_l, copies_r = [], []
    for side, raw, sem, copies in ((0, lraw, lsem, copies_l), (1, rraw, rsem, copies_r)):
        for k in range(SLOTS):
            device = p if k < 8 else p + 1 - 2 * c
            row = pl.multiple_of(pairs[side, (device * NY + y) * 8 + k % 8] * SH, SH)
            cp = pltpu.make_async_copy(coeffs.at[pl.ds(row, SH), :], raw.at[pl.ds(k * SH, SH), :], sem.at[k])
            cp.start()
            copies.append(cp)
    ip = lax.broadcasted_iota(jnp.int32, (256, 512), 0)
    col = lax.broadcasted_iota(jnp.int32, (256, 512), 1)
    want = (((ip >> 6) + x) & 3) * 128 + ((ip >> 3) & 7) * 16 + c * 8 + (ip & 7)
    sel = jnp.where(col == want, 1.0, 0.0).astype(BF)
    for cp in copies_l:
        cp.wait()
    for g in range(4):
        lt[g] = lax.dot_general(
            sel, lraw[pl.ds(g * 256, 256), :], (((1,), (1,)), ((), ())), preferred_element_type=F32
        ).astype(BF)
    for cp in copies_r:
        cp.wait()
    for yr in range(NY):
        col = pl.multiple_of(((y + yr) & (NY - 1)) * 128, 128)
        r[:, pl.ds(yr * 128, 128)] = rraw[:, pl.ds(col, 128)]


def panels(pairs, coeffs):
    return pl.pallas_call(
        panel_kernel,
        out_shape=tuple(jax.ShapeDtypeStruct(dims, BF) for dims in ((4, 256, 256), (1024, 512))),
        in_specs=[pl.BlockSpec(memory_space=pltpu.SMEM), pl.BlockSpec(memory_space=pl.ANY)],
        out_specs=(pl.BlockSpec(memory_space=pltpu.VMEM),) * 2,
        scratch_shapes=[
            pltpu.VMEM((1024, 512), BF),
            pltpu.VMEM((1024, 512), BF),
            pltpu.SemaphoreType.DMA((SLOTS,)),
            pltpu.SemaphoreType.DMA((SLOTS,)),
        ],
        compiler_params=pltpu.CompilerParams(vmem_limit_bytes=2 * VMEM),
        cost_estimate=pl.CostEstimate(flops=300_000_000, bytes_accessed=4_000_000, transcendentals=0),
        name="panels",
    )(pairs, coeffs)


def block_kernel(by_x, acc_at, plain_at, first_q, nq, own_n, mate_n, lt_ref, r, own_i, mate_i, earlier, far, plain, acc, own, lt, bd, half):
    slot = lax.broadcasted_iota(jnp.int32, (256, 256), 1) >> 6
    for g in range(4):
        keep = slot + 4 * (g % 2) < (own_n if g < 2 else mate_n)[0, 0]
        lt[g] = jnp.where(keep, lt_ref[g].astype(F32), 0.0).astype(BF)

    low = lax.broadcasted_iota(jnp.int32, (SH, 128), 1) < 64
    zero = jnp.zeros((SH, 128), F32)
    blank = jnp.zeros((SH, 128), BF)
    for two in range(nq // 2):
        for k in range(SLOTS):
            src = (own_i if k < 8 else mate_i)[k % 8, :, pl.ds((first_q + 2 * two) * 64, 128)].astype(F32)
            swapped = pltpu.roll(src, 64, 1)
            g, kk = k // 4, k % 4
            rows = pl.ds(kk * SH, SH)
            for odd in range(2):
                piece = src if (kk % 2) == odd else swapped
                piece = jnp.where(low, zero, piece) if kk % 2 else jnp.where(low, piece, zero)
                bd[2 * two + odd, g, rows, pl.ds((kk // 2) * 128, 128)] = piece.astype(BF)
                bd[2 * two + odd, g, rows, pl.ds((1 - kk // 2) * 128, 128)] = blank
    for q in range(nq):
        for g in range(4):
            half[pl.ds(q * 256, 256), pl.ds(g * 256, 256)] = jnp.dot(
                lt[g], bd[q, g], preferred_element_type=F32
            ).astype(BF)
    res = jnp.dot(half[...], r[...], preferred_element_type=F32)
    for q in range(nq):
        for at, ref in ((0, own), (2, far), (plain_at, plain), (acc_at, acc)):
            if by_x:
                part = res[q * 256 + at * 64 : q * 256 + at * 64 + 64, :]
            else:
                part = res[q * 256 : q * 256 + 256, at * 128 : at * 128 + 128]
            ref[q] = part.astype(ref.dtype)


def block(by_x, acc_at, plain_at, first_q, nq, earlier, own_n, mate_n, lt, r, own_i, mate_i):
    rows, cols = (64, 512) if by_x else (256, 128)
    out = lambda dt: jax.ShapeDtypeStruct((nq, rows, cols), dt)
    smem, vmem = pl.BlockSpec(memory_space=pltpu.SMEM), pl.BlockSpec(memory_space=pltpu.VMEM)
    return pl.pallas_call(
        functools.partial(block_kernel, by_x, acc_at, plain_at, first_q, nq),
        out_shape=(out(BF), out(BF), out(F32), out(F32)),
        in_specs=[smem, smem, vmem, vmem, vmem, vmem, pl.BlockSpec(memory_space=pl.ANY)],
        out_specs=(vmem,) * 4,
        scratch_shapes=[
            pltpu.VMEM((4, 256, 256), BF),
            pltpu.VMEM((nq, 4, 256, 256), BF),
            pltpu.VMEM((nq * 256, 1024), BF),
        ],
        compiler_params=pltpu.CompilerParams(vmem_limit_bytes=VMEM),
        cost_estimate=pl.CostEstimate(flops=1_000_000, bytes_accessed=10_000, transcendentals=0),
        name="block_x" if by_x else "block_y",
    )(own_n, mate_n, lt, r, own_i, mate_i, earlier)


def tie(*values):
    return lax.optimization_barrier(values)


def on_device(integrals, coeffs, shell_pairs, block_count):
    mate_i = swap_core(integrals)
    mate_n = swap_core(block_count)
    lt, r = panels(shell_pairs.T, coeffs)

    def parts(by_x, up, first_q, earlier, nq=6):
        acc_at, plain_at = (1, 3) if up else (3, 1)
        return block(by_x, acc_at, plain_at, first_q, nq, earlier, block_count, mate_n, lt, r, integrals, mate_i)

    def join(acc, far):
        return (acc + far.astype(F32)).astype(BF)

    def total(own, plain, acc):
        return own + plain.astype(F32) + acc.astype(F32)

    na, ma, nb, mb = SIZES
    far_xa, plain_xa, acc_xa, own_xa = parts(True, True, 0, lt, na)
    f_xa = move_x(far_xa, 1)
    p_xa = move_x(plain_xa, -1)
    far_ya, plain_ya, acc_ya, own_ya = parts(False, True, na + nb, own_xa, ma)
    f_ya = move_y(far_ya, 1)
    p_ya = move_y(plain_ya, -1)
    far_xb, plain_xb, acc_xb, own_xb = parts(True, False, na, own_ya, nb)
    far_xb, plain_xb, f_xa, p_xa, own_xb = tie(far_xb, plain_xb, f_xa, p_xa, own_xb)
    f_xb = move_x(far_xb, -1)
    p_xb = move_x(plain_xb, 1)
    far_yb, plain_yb, acc_yb, own_yb = parts(False, False, na + nb + ma, own_xb, mb)
    far_yb, plain_yb, f_ya, p_ya, own_yb = tie(far_yb, plain_yb, f_ya, p_ya, own_yb)
    f_yb = move_y(far_yb, -1)
    p_yb = move_y(plain_yb, 1)
    f_xa, f_xb, p_xb, own_yb, f_ya = tie(f_xa, f_xb, p_xb, own_yb, f_ya)
    a_xa = move_x(join(acc_xa, f_xa), 1)
    a_xb = move_x(join(acc_xb, f_xb), -1)
    a_ya = move_y(join(acc_ya, f_ya), 1)
    a_yb = move_y(join(acc_yb, f_yb), -1)
    sum_x = jnp.concatenate([total(own_xa, p_xa, a_xa), total(own_xb, p_xb, a_xb)], axis=0)
    sum_y = jnp.concatenate([total(own_ya, p_ya, a_ya), total(own_yb, p_yb, a_yb)], axis=0)

    sum_x, sum_y = tie(sum_x, sum_y)
    tot_x, tot_y = sum_x[:, :, :128], sum_y[:, :64, :]
    for d in (1, 3, 2):
        tot_x = tot_x + move_y(sum_x[:, :, d * 128 : d * 128 + 128].astype(BF), d).astype(F32)
        tot_y = tot_y + move_x(sum_y[:, d * 64 : d * 64 + 64, :].astype(BF), d).astype(F32)

    tot = jnp.concatenate([tot_x, tot_y], axis=0)
    send = jnp.transpose(tot.reshape(24, NZ, 8, 128), (1, 2, 0, 3))
    zi = (lax.axis_index("pair") // NC) % NZ
    own = lax.dynamic_index_in_dim(send, zi, 0, keepdims=False)
    got = trade_z(send.astype(BF))
    return jnp.where((jnp.arange(NZ) == zi)[:, None, None, None], own[None], got.astype(F32)).sum(0)


def solution(mesh):
    return jax.shard_map(
        on_device,
        mesh=mesh,
        in_specs=(P(("pair", "red"), None, None), P(), P(), P("pair", "red")),
        out_specs=P("pair", None, "red"),
        check_vma=False,
    )
```

```python
import functools

import jax
import jax.numpy as jnp
from jax import lax
from jax.experimental import pallas as pl
from jax.experimental.pallas import tpu as pltpu
from jax.sharding import PartitionSpec as P

NX, NZ, NC, NY = 4, 8, 2, 4
SLOTS = 16
SH = 64
BF, F32 = jnp.bfloat16, jnp.float32
VMEM = 24 * 1024 * 1024
SIZES = (6, 6, 6, 6)


def pair_of(x, z, c):
    return (x * NZ + z) * NC + c


COORDS = [(x, z, c) for x in range(NX) for z in range(NZ) for c in range(NC)]


def move_x(a, d):
    return lax.ppermute(a, "pair", [(pair_of(x, z, c), pair_of((x + d) % NX, z, c)) for x, z, c in COORDS])


def trade_z(a):
    groups = [[pair_of(x, z, c) for z in range(NZ)] for x in range(NX) for c in range(NC)]
    return lax.all_to_all(a, "pair", 0, 0, tiled=True, axis_index_groups=groups)


def move_y(a, d):
    return lax.ppermute(a, "red", [(y, (y + d) % NY) for y in range(NY)])


def swap_core(a):
    return lax.ppermute(a, "pair", [(pair_of(x, z, c), pair_of(x, z, 1 - c)) for x, z, c in COORDS])


def panel_kernel(pairs, coeffs, lt, r, lraw, rraw, lsem, rsem):
    p, y = lax.axis_index("pair"), lax.axis_index("red")
    x, c = p >> 4, p & 1
    copies_l, copies_r = [], []
    for side, raw, sem, copies in ((0, lraw, lsem, copies_l), (1, rraw, rsem, copies_r)):
        for k in range(SLOTS):
            device = p if k < 8 else p + 1 - 2 * c
            row = pl.multiple_of(pairs[side, (device * NY + y) * 8 + k % 8] * SH, SH)
            cp = pltpu.make_async_copy(coeffs.at[pl.ds(row, SH), :], raw.at[pl.ds(k * SH, SH), :], sem.at[k])
            cp.start()
            copies.append(cp)
    ip = lax.broadcasted_iota(jnp.int32, (256, 512), 0)
    col = lax.broadcasted_iota(jnp.int32, (256, 512), 1)
    want = (((ip >> 6) + x) & 3) * 128 + ((ip >> 3) & 7) * 16 + c * 8 + (ip & 7)
    sel = jnp.where(col == want, 1.0, 0.0).astype(BF)
    for cp in copies_l:
        cp.wait()
    for g in range(4):
        lt[g] = lax.dot_general(
            sel, lraw[pl.ds(g * 256, 256), :], (((1,), (1,)), ((), ())), preferred_element_type=F32
        ).astype(BF)
    for cp in copies_r:
        cp.wait()
    for yr in range(NY):
        col = pl.multiple_of(((y + yr) & (NY - 1)) * 128, 128)
        r[:, pl.ds(yr * 128, 128)] = rraw[:, pl.ds(col, 128)]


def panels(pairs, coeffs):
    return pl.pallas_call(
        panel_kernel,
        out_shape=tuple(jax.ShapeDtypeStruct(dims, BF) for dims in ((4, 256, 256), (1024, 512))),
        in_specs=[pl.BlockSpec(memory_space=pltpu.SMEM), pl.BlockSpec(memory_space=pl.ANY)],
        out_specs=(pl.BlockSpec(memory_space=pltpu.VMEM),) * 2,
        scratch_shapes=[
            pltpu.VMEM((1024, 512), BF),
            pltpu.VMEM((1024, 512), BF),
            pltpu.SemaphoreType.DMA((SLOTS,)),
            pltpu.SemaphoreType.DMA((SLOTS,)),
        ],
        compiler_params=pltpu.CompilerParams(vmem_limit_bytes=2 * VMEM),
        cost_estimate=pl.CostEstimate(flops=300_000_000, bytes_accessed=4_000_000, transcendentals=0),
        name="panels",
    )(pairs, coeffs)


def block_kernel(by_x, acc_at, plain_at, first_q, nq, own_n, mate_n, lt_ref, r, own_i, mate_i, earlier, far, plain, acc, own, lt, bd, half):
    slot = lax.broadcasted_iota(jnp.int32, (256, 256), 1) >> 6
    for g in range(4):
        keep = slot + 4 * (g % 2) < (own_n if g < 2 else mate_n)[0, 0]
        lt[g] = jnp.where(keep, lt_ref[g].astype(F32), 0.0).astype(BF)

    low = lax.broadcasted_iota(jnp.int32, (SH, 128), 1) < 64
    zero = jnp.zeros((SH, 128), F32)
    blank = jnp.zeros((SH, 128), BF)
    for two in range(nq // 2):
        for k in range(SLOTS):
            src = (own_i if k < 8 else mate_i)[k % 8, :, pl.ds((first_q + 2 * two) * 64, 128)].astype(F32)
            swapped = pltpu.roll(src, 64, 1)
            g, kk = k // 4, k % 4
            rows = pl.ds(kk * SH, SH)
            for odd in range(2):
                piece = src if (kk % 2) == odd else swapped
                piece = jnp.where(low, zero, piece) if kk % 2 else jnp.where(low, piece, zero)
                bd[2 * two + odd, g, rows, pl.ds((kk // 2) * 128, 128)] = piece.astype(BF)
                bd[2 * two + odd, g, rows, pl.ds((1 - kk // 2) * 128, 128)] = blank
    for q in range(nq):
        for g in range(4):
            half[pl.ds(q * 256, 256), pl.ds(g * 256, 256)] = jnp.dot(
                lt[g], bd[q, g], preferred_element_type=F32
            ).astype(BF)
    res = jnp.dot(half[...], r[...], preferred_element_type=F32)
    for q in range(nq):
        for at, ref in ((0, own), (2, far), (plain_at, plain), (acc_at, acc)):
            if by_x:
                part = res[q * 256 + at * 64 : q * 256 + at * 64 + 64, :]
            else:
                part = res[q * 256 : q * 256 + 256, at * 128 : at * 128 + 128]
            ref[q] = part.astype(ref.dtype)


def block(by_x, acc_at, plain_at, first_q, nq, earlier, own_n, mate_n, lt, r, own_i, mate_i):
    rows, cols = (64, 512) if by_x else (256, 128)
    out = lambda dt: jax.ShapeDtypeStruct((nq, rows, cols), dt)
    smem, vmem = pl.BlockSpec(memory_space=pltpu.SMEM), pl.BlockSpec(memory_space=pltpu.VMEM)
    return pl.pallas_call(
        functools.partial(block_kernel, by_x, acc_at, plain_at, first_q, nq),
        out_shape=(out(BF), out(BF), out(F32), out(F32)),
        in_specs=[smem, smem, vmem, vmem, vmem, vmem, pl.BlockSpec(memory_space=pl.ANY)],
        out_specs=(vmem,) * 4,
        scratch_shapes=[
            pltpu.VMEM((4, 256, 256), BF),
            pltpu.VMEM((nq, 4, 256, 256), BF),
            pltpu.VMEM((nq * 256, 1024), BF),
        ],
        compiler_params=pltpu.CompilerParams(vmem_limit_bytes=VMEM),
        cost_estimate=pl.CostEstimate(flops=1_000_000, bytes_accessed=10_000, transcendentals=0),
        name="block_x" if by_x else "block_y",
    )(own_n, mate_n, lt, r, own_i, mate_i, earlier)


def tie(*values):
    return lax.optimization_barrier(values)


def on_device(integrals, coeffs, shell_pairs, block_count):
    mate_i = swap_core(integrals)
    mate_n = swap_core(block_count)
    lt, r = panels(shell_pairs.T, coeffs)

    def parts(by_x, up, first_q, earlier, nq=6):
        acc_at, plain_at = (1, 3) if up else (3, 1)
        return block(by_x, acc_at, plain_at, first_q, nq, earlier, block_count, mate_n, lt, r, integrals, mate_i)

    def join(acc, far):
        return (acc + far.astype(F32)).astype(BF)

    def total(own, plain, acc):
        return own + plain.astype(F32) + acc.astype(F32)

    na, ma, nb, mb = SIZES
    far_xa, plain_xa, acc_xa, own_xa = parts(True, True, 0, lt, na)
    f_xa = move_x(far_xa, 1)
    p_xa = move_x(plain_xa, -1)
    far_ya, plain_ya, acc_ya, own_ya = parts(False, True, na + nb, own_xa, ma)
    f_ya = move_y(far_ya, 1)
    p_ya = move_y(plain_ya, -1)
    far_xb, plain_xb, acc_xb, own_xb = parts(True, False, na, own_ya, nb)
    plain_xb, f_xa, p_xa, own_xb = tie(plain_xb, f_xa, p_xa, own_xb)
    f_xb = move_x(far_xb, -1)
    p_xb = move_x(plain_xb, 1)
    far_yb, plain_yb, acc_yb, own_yb = parts(False, False, na + nb + ma, own_xb, mb)
    far_yb, plain_yb, f_ya, p_ya, own_yb = tie(far_yb, plain_yb, f_ya, p_ya, own_yb)
    f_yb = move_y(far_yb, -1)
    p_yb = move_y(plain_yb, 1)
    f_xa, f_xb, p_xb, own_yb = tie(f_xa, f_xb, p_xb, own_yb)
    a_xa = move_x(join(acc_xa, f_xa), 1)
    a_xb = move_x(join(acc_xb, f_xb), -1)
    a_ya = move_y(join(acc_ya, f_ya), 1)
    a_yb = move_y(join(acc_yb, f_yb), -1)
    sum_x = jnp.concatenate([total(own_xa, p_xa, a_xa), total(own_xb, p_xb, a_xb)], axis=0)
    sum_y = jnp.concatenate([total(own_ya, p_ya, a_ya), total(own_yb, p_yb, a_yb)], axis=0)

    sum_x, sum_y = tie(sum_x, sum_y)
    tot_x, tot_y = sum_x[:, :, :128], sum_y[:, :64, :]
    for d in (1, 3, 2):
        tot_x = tot_x + move_y(sum_x[:, :, d * 128 : d * 128 + 128].astype(BF), d).astype(F32)
        tot_y = tot_y + move_x(sum_y[:, d * 64 : d * 64 + 64, :].astype(BF), d).astype(F32)

    tot = jnp.concatenate([tot_x, tot_y], axis=0)
    send = jnp.transpose(tot.reshape(24, NZ, 8, 128), (1, 2, 0, 3))
    zi = (lax.axis_index("pair") // NC) % NZ
    own = lax.dynamic_index_in_dim(send, zi, 0, keepdims=False)
    got = trade_z(send.astype(BF))
    return jnp.where((jnp.arange(NZ) == zi)[:, None, None, None], own[None], got.astype(F32)).sum(0)


def solution(mesh):
    return jax.shard_map(
        on_device,
        mesh=mesh,
        in_specs=(P(("pair", "red"), None, None), P(), P(), P("pair", "red")),
        out_specs=P("pair", None, "red"),
        check_vma=False,
    )
```

```python
import functools

import jax
import jax.numpy as jnp
from jax import lax
from jax.experimental import pallas as pl
from jax.experimental.pallas import tpu as pltpu
from jax.sharding import PartitionSpec as P

NX, NZ, NC, NY = 4, 8, 2, 4
SLOTS = 16
SH = 64
BF, F32 = jnp.bfloat16, jnp.float32
VMEM = 24 * 1024 * 1024
SIZES = (6, 6, 6, 6)


def pair_of(x, z, c):
    return (x * NZ + z) * NC + c


COORDS = [(x, z, c) for x in range(NX) for z in range(NZ) for c in range(NC)]


def move_x(a, d):
    return lax.ppermute(a, "pair", [(pair_of(x, z, c), pair_of((x + d) % NX, z, c)) for x, z, c in COORDS])


def trade_z(a):
    groups = [[pair_of(x, z, c) for z in range(NZ)] for x in range(NX) for c in range(NC)]
    return lax.all_to_all(a, "pair", 0, 0, tiled=True, axis_index_groups=groups)


def move_y(a, d):
    return lax.ppermute(a, "red", [(y, (y + d) % NY) for y in range(NY)])


def swap_core(a):
    return lax.ppermute(a, "pair", [(pair_of(x, z, c), pair_of(x, z, 1 - c)) for x, z, c in COORDS])


def panel_kernel(pairs, coeffs, lt, r, lraw, rraw, lsem, rsem):
    p, y = lax.axis_index("pair"), lax.axis_index("red")
    x, c = p >> 4, p & 1
    copies_l, copies_r = [], []
    for side, raw, sem, copies in ((0, lraw, lsem, copies_l), (1, rraw, rsem, copies_r)):
        for k in range(SLOTS):
            device = p if k < 8 else p + 1 - 2 * c
            row = pl.multiple_of(pairs[side, (device * NY + y) * 8 + k % 8] * SH, SH)
            cp = pltpu.make_async_copy(coeffs.at[pl.ds(row, SH), :], raw.at[pl.ds(k * SH, SH), :], sem.at[k])
            cp.start()
            copies.append(cp)
    ip = lax.broadcasted_iota(jnp.int32, (256, 512), 0)
    col = lax.broadcasted_iota(jnp.int32, (256, 512), 1)
    want = (((ip >> 6) + x) & 3) * 128 + ((ip >> 3) & 7) * 16 + c * 8 + (ip & 7)
    sel = jnp.where(col == want, 1.0, 0.0).astype(BF)
    for cp in copies_l:
        cp.wait()
    for g in range(4):
        lt[g] = lax.dot_general(
            sel, lraw[pl.ds(g * 256, 256), :], (((1,), (1,)), ((), ())), preferred_element_type=F32
        ).astype(BF)
    for cp in copies_r:
        cp.wait()
    for yr in range(NY):
        col = pl.multiple_of(((y + yr) & (NY - 1)) * 128, 128)
        r[:, pl.ds(yr * 128, 128)] = rraw[:, pl.ds(col, 128)]


def panels(pairs, coeffs):
    return pl.pallas_call(
        panel_kernel,
        out_shape=tuple(jax.ShapeDtypeStruct(dims, BF) for dims in ((4, 256, 256), (1024, 512))),
        in_specs=[pl.BlockSpec(memory_space=pltpu.SMEM), pl.BlockSpec(memory_space=pl.ANY)],
        out_specs=(pl.BlockSpec(memory_space=pltpu.VMEM),) * 2,
        scratch_shapes=[
            pltpu.VMEM((1024, 512), BF),
            pltpu.VMEM((1024, 512), BF),
            pltpu.SemaphoreType.DMA((SLOTS,)),
            pltpu.SemaphoreType.DMA((SLOTS,)),
        ],
        compiler_params=pltpu.CompilerParams(vmem_limit_bytes=2 * VMEM),
        cost_estimate=pl.CostEstimate(flops=300_000_000, bytes_accessed=4_000_000, transcendentals=0),
        name="panels",
    )(pairs, coeffs)


def block_kernel(by_x, acc_at, plain_at, first_q, nq, own_n, mate_n, lt_ref, r, own_i, mate_i, earlier, far, plain, acc, own, lt, bd, half):
    slot = lax.broadcasted_iota(jnp.int32, (256, 256), 1) >> 6
    for g in range(4):
        keep = slot + 4 * (g % 2) < (own_n if g < 2 else mate_n)[0, 0]
        lt[g] = jnp.where(keep, lt_ref[g].astype(F32), 0.0).astype(BF)

    low = lax.broadcasted_iota(jnp.int32, (SH, 128), 1) < 64
    zero = jnp.zeros((SH, 128), F32)
    blank = jnp.zeros((SH, 128), BF)
    for two in range(nq // 2):
        for k in range(SLOTS):
            src = (own_i if k < 8 else mate_i)[k % 8, :, pl.ds((first_q + 2 * two) * 64, 128)].astype(F32)
            swapped = pltpu.roll(src, 64, 1)
            g, kk = k // 4, k % 4
            rows = pl.ds(kk * SH, SH)
            for odd in range(2):
                piece = src if (kk % 2) == odd else swapped
                piece = jnp.where(low, zero, piece) if kk % 2 else jnp.where(low, piece, zero)
                bd[2 * two + odd, g, rows, pl.ds((kk // 2) * 128, 128)] = piece.astype(BF)
                bd[2 * two + odd, g, rows, pl.ds((1 - kk // 2) * 128, 128)] = blank
    for q in range(nq):
        for g in range(4):
            half[pl.ds(q * 256, 256), pl.ds(g * 256, 256)] = jnp.dot(
                lt[g], bd[q, g], preferred_element_type=F32
            ).astype(BF)
    res = jnp.dot(half[...], r[...], preferred_element_type=F32)
    for q in range(nq):
        for at, ref in ((0, own), (2, far), (plain_at, plain), (acc_at, acc)):
            if by_x:
                part = res[q * 256 + at * 64 : q * 256 + at * 64 + 64, :]
            else:
                part = res[q * 256 : q * 256 + 256, at * 128 : at * 128 + 128]
            ref[q] = part.astype(ref.dtype)


def block(by_x, acc_at, plain_at, first_q, nq, earlier, own_n, mate_n, lt, r, own_i, mate_i):
    rows, cols = (64, 512) if by_x else (256, 128)
    out = lambda dt: jax.ShapeDtypeStruct((nq, rows, cols), dt)
    smem, vmem = pl.BlockSpec(memory_space=pltpu.SMEM), pl.BlockSpec(memory_space=pltpu.VMEM)
    return pl.pallas_call(
        functools.partial(block_kernel, by_x, acc_at, plain_at, first_q, nq),
        out_shape=(out(BF), out(BF), out(F32), out(F32)),
        in_specs=[smem, smem, vmem, vmem, vmem, vmem, pl.BlockSpec(memory_space=pl.ANY)],
        out_specs=(vmem,) * 4,
        scratch_shapes=[
            pltpu.VMEM((4, 256, 256), BF),
            pltpu.VMEM((nq, 4, 256, 256), BF),
            pltpu.VMEM((nq * 256, 1024), BF),
        ],
        compiler_params=pltpu.CompilerParams(vmem_limit_bytes=VMEM),
        cost_estimate=pl.CostEstimate(flops=1_000_000, bytes_accessed=10_000, transcendentals=0),
        name="block_x" if by_x else "block_y",
    )(own_n, mate_n, lt, r, own_i, mate_i, earlier)


def tie(*values):
    return lax.optimization_barrier(values)


def on_device(integrals, coeffs, shell_pairs, block_count):
    mate_i = swap_core(integrals)
    mate_n = swap_core(block_count)
    lt, r = panels(shell_pairs.T, coeffs)

    def parts(by_x, up, first_q, earlier, nq=6):
        acc_at, plain_at = (1, 3) if up else (3, 1)
        return block(by_x, acc_at, plain_at, first_q, nq, earlier, block_count, mate_n, lt, r, integrals, mate_i)

    def join(acc, far):
        return (acc + far.astype(F32)).astype(BF)

    def total(own, plain, acc):
        return own + plain.astype(F32) + acc.astype(F32)

    na, ma, nb, mb = SIZES
    far_xa, plain_xa, acc_xa, own_xa = parts(True, True, 0, lt, na)
    f_xa = move_x(far_xa, 1)
    p_xa = move_x(plain_xa, -1)
    far_ya, plain_ya, acc_ya, own_ya = parts(False, True, na + nb, own_xa, ma)
    f_ya = move_y(far_ya, 1)
    p_ya = move_y(plain_ya, -1)
    far_xb, plain_xb, acc_xb, own_xb = parts(True, False, na, own_ya, nb)
    plain_xb, f_xa, p_xa, own_xb = tie(plain_xb, f_xa, p_xa, own_xb)
    f_xb = move_x(far_xb, -1)
    p_xb = move_x(plain_xb, 1)
    far_yb, plain_yb, acc_yb, own_yb = parts(False, False, na + nb + ma, own_xb, mb)
    far_yb, plain_yb, f_ya, p_ya, own_yb = tie(far_yb, plain_yb, f_ya, p_ya, own_yb)
    f_yb = move_y(far_yb, -1)
    p_yb = move_y(plain_yb, 1)
    f_xa, f_xb, p_xb, own_yb = tie(f_xa, f_xb, p_xb, own_yb)
    a_xa = move_x(join(acc_xa, f_xa), 1)
    a_xb = move_x(join(acc_xb, f_xb), -1)
    a_ya = move_y(join(acc_ya, f_ya), 1)
    a_yb = move_y(join(acc_yb, f_yb), -1)
    sum_x = jnp.concatenate([total(own_xa, p_xa, a_xa), total(own_xb, p_xb, a_xb)], axis=0)
    sum_y = jnp.concatenate([total(own_ya, p_ya, a_ya), total(own_yb, p_yb, a_yb)], axis=0)

    sum_x, sum_y = tie(sum_x, sum_y)
    tot_x, tot_y = sum_x[:, :, :128], sum_y[:, :64, :]
    for d in (3, 1, 2):
        tot_x = tot_x + move_y(sum_x[:, :, d * 128 : d * 128 + 128].astype(BF), d).astype(F32)
        tot_y = tot_y + move_x(sum_y[:, d * 64 : d * 64 + 64, :].astype(BF), d).astype(F32)

    tot = jnp.concatenate([tot_x, tot_y], axis=0)
    send = jnp.transpose(tot.reshape(24, NZ, 8, 128), (1, 2, 0, 3))
    zi = (lax.axis_index("pair") // NC) % NZ
    own = lax.dynamic_index_in_dim(send, zi, 0, keepdims=False)
    got = trade_z(send.astype(BF))
    return jnp.where((jnp.arange(NZ) == zi)[:, None, None, None], own[None], got.astype(F32)).sum(0)


def solution(mesh):
    return jax.shard_map(
        on_device,
        mesh=mesh,
        in_specs=(P(("pair", "red"), None, None), P(), P(), P("pair", "red")),
        out_specs=P("pair", None, "red"),
        check_vma=False,
    )
```

```python
import functools

import jax
import jax.numpy as jnp
from jax import lax
from jax.experimental import pallas as pl
from jax.experimental.pallas import tpu as pltpu
from jax.sharding import PartitionSpec as P

NX, NZ, NC, NY = 4, 8, 2, 4
SLOTS = 16
SH = 64
BF, F32 = jnp.bfloat16, jnp.float32
VMEM = 24 * 1024 * 1024
SIZES = (6, 6, 6, 6)


def pair_of(x, z, c):
    return (x * NZ + z) * NC + c


COORDS = [(x, z, c) for x in range(NX) for z in range(NZ) for c in range(NC)]


def move_x(a, d):
    return lax.ppermute(a, "pair", [(pair_of(x, z, c), pair_of((x + d) % NX, z, c)) for x, z, c in COORDS])


def trade_z(a):
    groups = [[pair_of(x, z, c) for z in range(NZ)] for x in range(NX) for c in range(NC)]
    return lax.all_to_all(a, "pair", 0, 0, tiled=True, axis_index_groups=groups)


def move_y(a, d):
    return lax.ppermute(a, "red", [(y, (y + d) % NY) for y in range(NY)])


def swap_core(a):
    return lax.ppermute(a, "pair", [(pair_of(x, z, c), pair_of(x, z, 1 - c)) for x, z, c in COORDS])


def panel_kernel(pairs, coeffs, lt, r, lraw, rraw, lsem, rsem):
    p, y = lax.axis_index("pair"), lax.axis_index("red")
    x, c = p >> 4, p & 1
    copies_l, copies_r = [], []
    for side, raw, sem, copies in ((0, lraw, lsem, copies_l), (1, rraw, rsem, copies_r)):
        for k in range(SLOTS):
            device = p if k < 8 else p + 1 - 2 * c
            row = pl.multiple_of(pairs[side, (device * NY + y) * 8 + k % 8] * SH, SH)
            cp = pltpu.make_async_copy(coeffs.at[pl.ds(row, SH), :], raw.at[pl.ds(k * SH, SH), :], sem.at[k])
            cp.start()
            copies.append(cp)
    ip = lax.broadcasted_iota(jnp.int32, (256, 512), 0)
    col = lax.broadcasted_iota(jnp.int32, (256, 512), 1)
    want = (((ip >> 6) + x) & 3) * 128 + ((ip >> 3) & 7) * 16 + c * 8 + (ip & 7)
    sel = jnp.where(col == want, 1.0, 0.0).astype(BF)
    for cp in copies_l:
        cp.wait()
    for g in range(4):
        lt[g] = lax.dot_general(
            sel, lraw[pl.ds(g * 256, 256), :], (((1,), (1,)), ((), ())), preferred_element_type=F32
        ).astype(BF)
    for cp in copies_r:
        cp.wait()
    for yr in range(NY):
        col = pl.multiple_of(((y + yr) & (NY - 1)) * 128, 128)
        r[:, pl.ds(yr * 128, 128)] = rraw[:, pl.ds(col, 128)]


def panels(pairs, coeffs):
    return pl.pallas_call(
        panel_kernel,
        out_shape=tuple(jax.ShapeDtypeStruct(dims, BF) for dims in ((4, 256, 256), (1024, 512))),
        in_specs=[pl.BlockSpec(memory_space=pltpu.SMEM), pl.BlockSpec(memory_space=pl.ANY)],
        out_specs=(pl.BlockSpec(memory_space=pltpu.VMEM),) * 2,
        scratch_shapes=[
            pltpu.VMEM((1024, 512), BF),
            pltpu.VMEM((1024, 512), BF),
            pltpu.SemaphoreType.DMA((SLOTS,)),
            pltpu.SemaphoreType.DMA((SLOTS,)),
        ],
        compiler_params=pltpu.CompilerParams(vmem_limit_bytes=2 * VMEM),
        cost_estimate=pl.CostEstimate(flops=300_000_000, bytes_accessed=4_000_000, transcendentals=0),
        name="panels",
    )(pairs, coeffs)


def block_kernel(by_x, acc_at, plain_at, first_q, nq, own_n, mate_n, lt_ref, r, own_i, mate_i, earlier, far, plain, acc, own, lt, bd, half):
    slot = lax.broadcasted_iota(jnp.int32, (256, 256), 1) >> 6
    for g in range(4):
        keep = slot + 4 * (g % 2) < (own_n if g < 2 else mate_n)[0, 0]
        lt[g] = jnp.where(keep, lt_ref[g].astype(F32), 0.0).astype(BF)

    low = lax.broadcasted_iota(jnp.int32, (SH, 128), 1) < 64
    zero = jnp.zeros((SH, 128), BF)
    for two in range(nq // 2):
        for k in range(SLOTS):
            src = (own_i if k < 8 else mate_i)[k % 8, :, pl.ds((first_q + 2 * two) * 64, 128)]
            swapped = pltpu.roll(src, 64, 1)
            g, kk = k // 4, k % 4
            rows = pl.ds(kk * SH, SH)
            for odd in range(2):
                piece = src if (kk % 2) == odd else swapped
                piece = jnp.where(low, zero, piece) if kk % 2 else jnp.where(low, piece, zero)
                bd[2 * two + odd, g, rows, pl.ds((kk // 2) * 128, 128)] = piece
                bd[2 * two + odd, g, rows, pl.ds((1 - kk // 2) * 128, 128)] = zero
    for q in range(nq):
        for g in range(4):
            half[pl.ds(q * 256, 256), pl.ds(g * 256, 256)] = jnp.dot(
                lt[g], bd[q, g], preferred_element_type=F32
            ).astype(BF)
    res = jnp.dot(half[...], r[...], preferred_element_type=F32)
    for q in range(nq):
        for at, ref in ((0, own), (2, far), (plain_at, plain), (acc_at, acc)):
            if by_x:
                part = res[q * 256 + at * 64 : q * 256 + at * 64 + 64, :]
            else:
                part = res[q * 256 : q * 256 + 256, at * 128 : at * 128 + 128]
            ref[q] = part.astype(ref.dtype)


def block(by_x, acc_at, plain_at, first_q, nq, earlier, own_n, mate_n, lt, r, own_i, mate_i):
    rows, cols = (64, 512) if by_x else (256, 128)
    out = lambda dt: jax.ShapeDtypeStruct((nq, rows, cols), dt)
    smem, vmem = pl.BlockSpec(memory_space=pltpu.SMEM), pl.BlockSpec(memory_space=pltpu.VMEM)
    return pl.pallas_call(
        functools.partial(block_kernel, by_x, acc_at, plain_at, first_q, nq),
        out_shape=(out(BF), out(BF), out(F32), out(F32)),
        in_specs=[smem, smem, vmem, vmem, vmem, vmem, pl.BlockSpec(memory_space=pl.ANY)],
        out_specs=(vmem,) * 4,
        scratch_shapes=[
            pltpu.VMEM((4, 256, 256), BF),
            pltpu.VMEM((nq, 4, 256, 256), BF),
            pltpu.VMEM((nq * 256, 1024), BF),
        ],
        compiler_params=pltpu.CompilerParams(vmem_limit_bytes=VMEM),
        cost_estimate=pl.CostEstimate(flops=1_000_000, bytes_accessed=10_000, transcendentals=0),
        name="block_x" if by_x else "block_y",
    )(own_n, mate_n, lt, r, own_i, mate_i, earlier)


def tie(*values):
    return lax.optimization_barrier(values)


def on_device(integrals, coeffs, shell_pairs, block_count):
    mate_i = swap_core(integrals)
    mate_n = swap_core(block_count)
    lt, r = panels(shell_pairs.T, coeffs)

    def parts(by_x, up, first_q, earlier, nq=6):
        acc_at, plain_at = (1, 3) if up else (3, 1)
        return block(by_x, acc_at, plain_at, first_q, nq, earlier, block_count, mate_n, lt, r, integrals, mate_i)

    def join(acc, far):
        return (acc + far.astype(F32)).astype(BF)

    def total(own, plain, acc):
        return own + plain.astype(F32) + acc.astype(F32)

    na, ma, nb, mb = SIZES
    far_xa, plain_xa, acc_xa, own_xa = parts(True, True, 0, lt, na)
    f_xa = move_x(far_xa, 1)
    p_xa = move_x(plain_xa, -1)
    far_ya, plain_ya, acc_ya, own_ya = parts(False, True, na + nb, own_xa, ma)
    f_ya = move_y(far_ya, 1)
    p_ya = move_y(plain_ya, -1)
    far_xb, plain_xb, acc_xb, own_xb = parts(True, False, na, own_ya, nb)
    plain_xb, f_xa, p_xa, own_xb = tie(plain_xb, f_xa, p_xa, own_xb)
    f_xb = move_x(far_xb, -1)
    p_xb = move_x(plain_xb, 1)
    far_yb, plain_yb, acc_yb, own_yb = parts(False, False, na + nb + ma, own_xb, mb)
    plain_yb, f_ya, p_ya, own_yb = tie(plain_yb, f_ya, p_ya, own_yb)
    f_yb = move_y(far_yb, -1)
    p_yb = move_y(plain_yb, 1)
    f_xa, f_xb, p_xb, own_yb = tie(f_xa, f_xb, p_xb, own_yb)
    a_xa = move_x(join(acc_xa, f_xa), 1)
    a_xb = move_x(join(acc_xb, f_xb), -1)
    a_ya = move_y(join(acc_ya, f_ya), 1)
    a_yb = move_y(join(acc_yb, f_yb), -1)
    sum_x = jnp.concatenate([total(own_xa, p_xa, a_xa), total(own_xb, p_xb, a_xb)], axis=0)
    sum_y = jnp.concatenate([total(own_ya, p_ya, a_ya), total(own_yb, p_yb, a_yb)], axis=0)

    sum_x, sum_y = tie(sum_x, sum_y)
    tot_x, tot_y = sum_x[:, :, :128], sum_y[:, :64, :]
    for d in (3, 1, 2):
        tot_x = tot_x + move_y(sum_x[:, :, d * 128 : d * 128 + 128].astype(BF), d).astype(F32)
        tot_y = tot_y + move_x(sum_y[:, d * 64 : d * 64 + 64, :].astype(BF), d).astype(F32)

    tot = jnp.concatenate([tot_x, tot_y], axis=0)
    send = jnp.transpose(tot.reshape(24, NZ, 8, 128), (1, 2, 0, 3))
    zi = (lax.axis_index("pair") // NC) % NZ
    own = lax.dynamic_index_in_dim(send, zi, 0, keepdims=False)
    got = trade_z(send.astype(BF))
    return jnp.where((jnp.arange(NZ) == zi)[:, None, None, None], own[None], got.astype(F32)).sum(0)


def solution(mesh):
    return jax.shard_map(
        on_device,
        mesh=mesh,
        in_specs=(P(("pair", "red"), None, None), P(), P(), P("pair", "red")),
        out_specs=P("pair", None, "red"),
        check_vma=False,
    )
```
